1024 devices in a mesh: rep: 128 (over y_hi, z, core), fsdp: 8 (over x, y_lo).
Axes of the slice: x: 4, y: 4 (y_hi: 2, y_lo: 2; y = y_hi * 2 + y_lo), z: 32, core: 2. Of those that a mesh axis runs over, the one named last changes fastest.
Arguments:
- activations: bfloat16 [65536, 8192], P('rep'), may hold values from -6 to 6
- key_cotangent: bfloat16 [65536, 1024], P('rep', 'fsdp'), may hold values from -0.25 to 0.25
- deltas: bfloat16 [128, 512, 1024], P('rep', None, 'fsdp'), may hold values from -24 to 24
- delta_scales: int32 [128, 512, 8], P('rep', None, 'fsdp'), may hold values from -3 to 0
- global_copy: float32 [512, 1024], P(None, 'fsdp'), may hold values from -0.75 to 0.75
- momentum: float32 [512, 1024], P(None, 'fsdp'), may hold values from -0.75 to 0.75
- code_scales: int32 [512, 8], P(None, 'fsdp'), may hold values from -6 to -3
Outputs:
- key_grad: bfloat16 [128, 8192, 1024], P('rep', None, 'fsdp')
- new_momentum: float32 [512, 1024], P('rep', 'fsdp')
- new_global: float32 [512, 1024], P('rep', 'fsdp')
- encoded: bfloat16 [512, 1024], P(None, 'fsdp')
The draws below stay inside these ranges and needn't reach their ends.
All inputs are finite; a program needn't handle non-finite values.
Results may differ from the reference program's by a relative error of at most 0.001.
Values may be sent and summed in bfloat16 or wider, within the bound.
No kernel may reach another device: no remote copies, remote signals or barrier semaphores. Data moves between devices by JAX's collectives and lax.ppermute only.
A program may use at most 32 MiB of HBM per device.

```python
import jax
import jax.numpy as jnp
from jax import lax

D = 8192
KV = 1024
TOK = 512
ROWS = 512
COLS = 1024
N_REP = 128


def place_ends(values, stream_key, smallest, top_value):
    index_at = [jax.random.randint(jax.random.fold_in(stream_key, axis), (), 0, length) for axis, length in enumerate(values.shape)]
    widest = values.shape.index(max(values.shape))
    beside = index_at[:widest] + [(index_at[widest] + 1) % values.shape[widest]] + index_at[widest + 1:]
    return values.at[tuple(index_at)].set(smallest).at[tuple(beside)].set(top_value)


def spiked(array, own_key, source, target, blocks, factor):
    owner, partner = [(jnp.arange(array.shape[axis_at]) // (array.shape[axis_at] // blocks)).reshape([-1 if axis == axis_at else 1 for axis in range(array.ndim)]) for axis_at in (source, target)]
    chosen = jax.random.permutation(own_key, blocks)[partner]
    strong = (owner == chosen) | (owner == (partner + blocks // 2) % blocks)
    return jnp.where(strong, factor * array, array)


def level_of(rng, extent, split, low, top_value):
    def one(position, parts):
        draws = jax.random.uniform(jax.random.fold_in(jax.random.fold_in(rng, 6), position), (parts,), jnp.float32, low / len(split), top_value / len(split))
        return jnp.repeat(jnp.exp(draws), extent[position] // parts).reshape((-1,) + (1,) * (len(extent) - position - 1))

    gain = one(*split[0])
    for cut in split[1:]:
        gain = gain * one(*cut)
    return gain


def bell_draw(stream_key, extent, deviation, bound, shards=(), kind=jnp.bfloat16):
    level = level_of(stream_key, extent, shards, -0.22, 0.18) if shards else 1.0
    result = jax.random.normal(stream_key, extent, jnp.float32) * deviation * level
    return jnp.minimum(jnp.maximum(result, -bound), bound).astype(kind)


def noise_with(rng, shape, spread, limit, cuts, heavy, kind=jnp.bfloat16):
    entries = spread * jax.random.normal(rng, shape, jnp.float32)
    if cuts:
        entries = entries * level_of(rng, shape, cuts, -0.22, 0.18)
    return jnp.clip(spiked(entries, jax.random.fold_in(rng, 3), *heavy), -limit, limit).astype(kind)


def setup_inputs(seed: int = 0) -> dict:
    key_of = jax.random.split(jax.random.key(seed), 8)
    activations = bell_draw(key_of[0], (N_REP * TOK, D), 1.0, 6.0, ((0, 128),))
    key_cotangent = bell_draw(key_of[1], (N_REP * TOK, KV), TOK ** -0.5, 0.25, ((0, 128), (1, 8)))
    deltas = noise_with(key_of[2], (N_REP, ROWS, COLS), 1.0, 24.0, ((0, 128), (2, 8)), (0, 1, 128, 5.5))
    delta_scales = place_ends(jax.random.randint(key_of[3], (N_REP, ROWS, COLS // 128), -3, 1), jax.random.fold_in(key_of[3], 1), -3, 0).astype(jnp.int32)
    global_copy = bell_draw(key_of[4], (ROWS, COLS), 0.05, 0.75, ((1, 8),), jnp.float32)
    momentum = bell_draw(key_of[5], (ROWS, COLS), 0.05, 0.75, ((1, 8),), jnp.float32)
    code_scales = place_ends(jax.random.randint(key_of[6], (ROWS, COLS // 128), -6, -2), jax.random.fold_in(key_of[6], 1), -6, (-2) - 1).astype(jnp.int32)
    return {"activations": activations, "key_cotangent": key_cotangent, "deltas": deltas, "delta_scales": delta_scales, "global_copy": global_copy, "momentum": momentum, "code_scales": code_scales}


outer_rate = 0.7
decay_rate = 0.9

def decode_block(coded, scales):
    row_count = coded.shape[0]
    blocked = coded.astype(jnp.float32).reshape(row_count, -1, 128)
    blocked = blocked * jnp.exp2(scales.astype(jnp.float32))[:, :, None]
    return blocked.reshape(row_count, -1)

def weight_grad(pair):
    return jnp.dot(pair[0].T, pair[1], preferred_element_type=jnp.float32).astype(jnp.bfloat16)

def reference(activations, key_cotangent, deltas, delta_scales, global_copy, momentum, code_scales):
    inputs = activations.reshape(N_REP, TOK, D)
    cotangent = key_cotangent.reshape(N_REP, TOK, KV)
    key_grad = lax.map(weight_grad, (inputs, cotangent))

    def accumulate(carry, pair):
        return (carry + decode_block(pair[0], pair[1]), None)
    summed, unused = lax.scan(accumulate, jnp.zeros((ROWS, COLS), jnp.float32), (deltas, delta_scales))
    outer_grad = -summed / N_REP
    new_momentum = decay_rate * momentum + outer_grad
    new_global = global_copy - outer_rate * (outer_grad + decay_rate * new_momentum)
    encoded = decode_block(new_global, -code_scales).astype(jnp.bfloat16)
    return (key_grad, new_momentum, new_global, encoded)
```

```python
import jax
import jax.numpy as jnp
import numpy as np
from jax import lax
from jax.sharding import Mesh, PartitionSpec as P

outer_rate = 0.7
decay_rate = 0.9

ZH, ZL = 4, 8
NEAR = ("yh", "zl", "core")
REP = ("yh", "zh", "zl", "core")


def powers(exponents):
    return jnp.exp2(exponents.astype(jnp.float32)).astype(jnp.bfloat16).astype(jnp.float32)


def shards(activations, key_cotangent, deltas, delta_scales, global_copy, momentum, code_scales):
    yh, zh, zl, core = [lax.axis_index(name) for name in REP]
    rows, columns = global_copy.shape
    sub = rows // (4 * ZH * ZL)

    decoded = deltas[0].astype(jnp.float32) * powers(delta_scales[0])
    decoded = decoded.astype(jnp.bfloat16).reshape(2, ZH, ZL, 2, sub, columns)
    outgoing = decoded.transpose(0, 2, 3, 1, 4, 5).reshape(rows, columns)
    incoming = lax.all_to_all(outgoing, NEAR, 0, 0, tiled=True)
    near_sum = jnp.sum(incoming.reshape(4 * ZL, ZH * sub, columns).astype(jnp.float32), axis=0)
    summed = lax.psum(near_sum, "zh").reshape(ZH, sub, columns)

    def own(array):
        split = array.reshape(2, ZH, ZL, 2, sub, array.shape[-1])
        part = lax.dynamic_slice(split, (yh, 0, zl, core, 0, 0), (1, ZH, 1, 1, sub, array.shape[-1]))
        return part.reshape(ZH, sub, array.shape[-1])

    outer_grad = -summed / lax.axis_size(REP)
    new_momentum = decay_rate * own(momentum) + outer_grad
    new_global = own(global_copy) - outer_rate * (outer_grad + decay_rate * new_momentum)
    coded = (new_global * powers(-own(code_scales))).astype(jnp.bfloat16)
    spread = jnp.broadcast_to(coded[None], (4 * ZL, ZH, sub, columns)).reshape(rows, columns)
    encoded = lax.all_to_all(spread, NEAR, 0, 0, tiled=True)
    encoded = encoded.reshape(2, ZL, 2, ZH, sub, columns).transpose(0, 3, 1, 2, 4, 5).reshape(rows, columns)

    key_grad = lax.dot_general(
        activations, key_cotangent, (((0,), (0,)), ((), ())), preferred_element_type=jnp.float32
    )
    key_grad = key_grad.astype(jnp.bfloat16)[None]
    pick = lambda array: lax.dynamic_index_in_dim(array, zh, 0, keepdims=False)
    return (key_grad, pick(new_momentum), pick(new_global), encoded)


def solution(mesh):
    devices = mesh.devices
    grid = Mesh(devices.reshape(2, ZH, ZL, 2, devices.shape[1]), (*REP, "fsdp"))
    in_specs = (
        P(REP, None),
        P(REP, "fsdp"),
        P(REP, None, "fsdp"),
        P(REP, None, "fsdp"),
        P(None, "fsdp"),
        P(None, "fsdp"),
        P(None, "fsdp"),
    )
    out_specs = (P(REP, None, "fsdp"), P(REP, "fsdp"), P(REP, "fsdp"), P(None, "fsdp"))
    return jax.shard_map(shards, mesh=grid, in_specs=in_specs, out_specs=out_specs, check_vma=False)
```

```python
import jax
import jax.numpy as jnp
from jax import lax
from jax.experimental import pallas as pl
from jax.experimental.pallas import tpu as pltpu
from jax.sharding import PartitionSpec as P

outer_rate = 0.7
decay_rate = 0.9

QUADS, LANES = 4, 8
RING = QUADS * LANES


def member(y_hi, z, core):
    return (y_hi * RING + z % RING) * 2 + core


STEPS = (0, -4, -3, -2, 3, -1, 2, 1)
BACK_STEPS = (0, 1, 2, 3, 4, -3, -2, -1)


def near(steps):
    return [
        [member(y, LANES * quad + step, core) for step in steps for y in (0, 1) for core in (0, 1)]
        for quad in range(QUADS)
    ]


NEAR, BACK = near(STEPS), near(BACK_STEPS)
FAR = [
    [member(y, first + LANES * quad, core) for quad in range(QUADS)]
    for first in (16, 17, 18, 19, 12, 13, 14, 15) for y in (0, 1) for core in (0, 1)
]


def powers(exponents):
    return jnp.exp2(exponents.astype(jnp.float32)).astype(jnp.bfloat16).astype(jnp.float32)


def decode(codes_ref, exponents_ref, out_ref):
    scales = powers(exponents_ref[...])
    block = scales.shape[1]
    rows = []
    for first in range(scales.shape[0]):
        turned = jnp.broadcast_to(scales[first : first + 1], (block, block)).T
        codes = codes_ref[pl.ds(first * block, block), :].astype(jnp.float32)
        rows.append((codes * turned).reshape(block // 8, 8, block))
    tiles = [part[i] for part in rows for i in range(block // 8)]
    low = lax.broadcasted_iota(jnp.int32, tiles[0].shape, 0) < 4
    for place, step in enumerate(STEPS):
        lane = step % LANES
        for y_hi in range(2):
            a, b, c, d = [tiles[(y_hi * QUADS + quad) * LANES + lane] for quad in range(QUADS)]
            first = (place * 2 + y_hi) * 2 * 16
            for core, (even, odd) in enumerate((((a, c), (b, d)), ((a, c), (b, d)))):
                halves = []
                for one, two in zip(even, odd):
                    if core == 0:
                        halves.append(jnp.where(low, one, pltpu.roll(two, 4, 0)))
                    else:
                        halves.append(jnp.where(low, pltpu.roll(one, 4, 0), two))
                out_ref[pl.ds(first + core * 16, 16), :] = jnp.concatenate(halves, axis=0).astype(jnp.bfloat16)


def shards(activations, key_cotangent, deltas, delta_scales, global_copy, momentum, code_scales):
    rep = lax.axis_index("rep")
    y_hi, z, core = rep // (2 * RING), (rep // 2) % RING, rep % 2
    quad, lane = z // LANES, z % LANES
    rows, columns = global_copy.shape
    sub = rows // (4 * RING)
    held = QUADS * sub

    def own(array):
        split = array.reshape(2, QUADS, LANES, 2, sub, array.shape[-1])
        part = lax.dynamic_slice(split, (y_hi, 0, lane, core, 0, 0), (1, QUADS, 1, 1, sub, array.shape[-1]))
        return part.reshape(QUADS, sub, array.shape[-1])

    scales = jnp.broadcast_to(powers(-own(code_scales)), (QUADS, sub, columns)).reshape(held, columns)
    outgoing = pl.pallas_call(
        decode,
        out_shape=jax.ShapeDtypeStruct((rows, columns), jnp.bfloat16),
        in_specs=[pl.BlockSpec(memory_space=pltpu.VMEM)] * 2,
        out_specs=pl.BlockSpec(memory_space=pltpu.VMEM),
        cost_estimate=pl.CostEstimate(flops=rows * columns, bytes_accessed=4 * rows * columns, transcendentals=rows),
    )(deltas[0], delta_scales.reshape(rows // columns, columns))
    outgoing, key_cotangent = lax.optimization_barrier((outgoing, key_cotangent))
    incoming = lax.all_to_all(outgoing, "rep", 0, 0, tiled=True, axis_index_groups=NEAR)
    key_grad = lax.dot_general(
        activations, key_cotangent, (((0,), (0,)), ((), ())), preferred_element_type=jnp.float32
    )
    key_grad = key_grad.astype(jnp.bfloat16)[None]
    incoming, key_grad, moment, base, scales = lax.optimization_barrier(
        (incoming, key_grad, own(momentum), own(global_copy), scales)
    )
    near_sum = jnp.sum(incoming.reshape(4 * LANES, held, columns).astype(jnp.float32), axis=0)
    sums = lax.psum(near_sum, "rep", axis_index_groups=FAR)
    def step(total, moment, base):
        outer_grad = -total / lax.axis_size("rep")
        new_momentum = decay_rate * moment + outer_grad
        return new_momentum, base - outer_rate * (outer_grad + decay_rate * new_momentum)

    moment, base = moment.reshape(held, columns), base.reshape(held, columns)
    copies = lambda array: jnp.broadcast_to(array[None], (4 * LANES, held, columns))
    spread = step(copies(sums), copies(moment), copies(base))[1] * copies(scales)
    spread = spread.astype(jnp.bfloat16).reshape(rows, columns)
    encoded = lax.all_to_all(spread, "rep", 0, 0, tiled=True, axis_index_groups=BACK)
    encoded = encoded.reshape(LANES, 2, 2, QUADS, sub, columns).transpose(1, 3, 0, 2, 4, 5).reshape(rows, columns)

    new_momentum, new_global = step(*[lax.dynamic_slice_in_dim(a, quad * sub, sub, 0) for a in (sums, moment, base)])
    return (key_grad, new_momentum, new_global, encoded)


def solution(mesh):
    in_specs = (
        P("rep", None),
        P("rep", "fsdp"),
        P("rep", None, "fsdp"),
        P("rep", None, "fsdp"),
        P(None, "fsdp"),
        P(None, "fsdp"),
        P(None, "fsdp"),
    )
    out_specs = (P("rep", None, "fsdp"), P("rep", "fsdp"), P("rep", "fsdp"), P(None, "fsdp"))
    return jax.shard_map(shards, mesh=mesh, in_specs=in_specs, out_specs=out_specs, check_vma=False)
```

```python
import jax
import jax.numpy as jnp
from jax import lax
from jax.experimental import pallas as pl
from jax.experimental.pallas import tpu as pltpu
from jax.sharding import PartitionSpec as P

outer_rate = 0.7
decay_rate = 0.9

QUADS, LANES = 4, 8
RING = QUADS * LANES


def member(y_hi, z, core):
    return (y_hi * RING + z % RING) * 2 + core


MIDDLE = 4
STEPS = (0, -4, -3, -2, 3, -1, 2, 1)
BACK_STEPS = (0, 1, 2, 3, -4, -3, -2, -1)


def near(steps, middle):
    return [
        [member(y, LANES * quad + middle + step, core) for step in steps for y in (0, 1) for core in (0, 1)]
        for quad in range(QUADS)
    ]


NEAR, BACK = near(STEPS, MIDDLE), near(BACK_STEPS, MIDDLE)
FAR = [
    [member(y, 2 * LANES + lane + LANES * quad, core) for quad in range(QUADS)]
    for lane in range(LANES) for y in (0, 1) for core in (0, 1)
]


def powers(exponents):
    return jnp.exp2(exponents.astype(jnp.float32)).astype(jnp.bfloat16).astype(jnp.float32)


def decode(codes_ref, exponents_ref, out_ref):
    scales = powers(exponents_ref[...])
    block = scales.shape[1]
    rows = []
    for first in range(scales.shape[0]):
        turned = jnp.broadcast_to(scales[first : first + 1], (block, block)).T
        codes = codes_ref[pl.ds(first * block, block), :].astype(jnp.float32)
        rows.append((codes * turned).reshape(block // 8, 8, block))
    tiles = [part[i] for part in rows for i in range(block // 8)]
    low = lax.broadcasted_iota(jnp.int32, tiles[0].shape, 0) < 4
    for place, step in enumerate(STEPS):
        lane = (MIDDLE + step) % LANES
        for y_hi in range(2):
            a, b, c, d = [tiles[(y_hi * QUADS + quad) * LANES + lane] for quad in range(QUADS)]
            first = (place * 2 + y_hi) * 2 * 16
            for core, (even, odd) in enumerate((((a, c), (b, d)), ((a, c), (b, d)))):
                halves = []
                for one, two in zip(even, odd):
                    if core == 0:
                        halves.append(jnp.where(low, one, pltpu.roll(two, 4, 0)))
                    else:
                        halves.append(jnp.where(low, pltpu.roll(one, 4, 0), two))
                out_ref[pl.ds(first + core * 16, 16), :] = jnp.concatenate(halves, axis=0).astype(jnp.bfloat16)


def shards(activations, key_cotangent, deltas, delta_scales, global_copy, momentum, code_scales):
    rep = lax.axis_index("rep")
    y_hi, z, core = rep // (2 * RING), (rep // 2) % RING, rep % 2
    quad, lane = z // LANES, z % LANES
    rows, columns = global_copy.shape
    sub = rows // (4 * RING)
    held = QUADS * sub

    def own(array):
        split = array.reshape(2, QUADS, LANES, 2, sub, array.shape[-1])
        part = lax.dynamic_slice(split, (y_hi, 0, lane, core, 0, 0), (1, QUADS, 1, 1, sub, array.shape[-1]))
        return part.reshape(QUADS, sub, array.shape[-1])

    scales = jnp.broadcast_to(powers(-own(code_scales)), (QUADS, sub, columns)).reshape(held, columns)
    outgoing = pl.pallas_call(
        decode,
        out_shape=jax.ShapeDtypeStruct((rows, columns), jnp.bfloat16),
        in_specs=[pl.BlockSpec(memory_space=pltpu.VMEM)] * 2,
        out_specs=pl.BlockSpec(memory_space=pltpu.VMEM),
        cost_estimate=pl.CostEstimate(flops=rows * columns, bytes_accessed=4 * rows * columns, transcendentals=rows),
    )(deltas[0], delta_scales.reshape(rows // columns, columns))
    incoming = lax.all_to_all(outgoing, "rep", 0, 0, tiled=True, axis_index_groups=NEAR)
    incoming, moment, base, scales = lax.optimization_barrier((incoming, own(momentum), own(global_copy), scales))
    near_sum = jnp.sum(incoming.reshape(4 * LANES, held, columns).astype(jnp.float32), axis=0)
    spread = jnp.broadcast_to(near_sum[None], (QUADS, held, columns)).reshape(QUADS * held, columns)
    parts = lax.all_to_all(spread, "rep", 0, 0, tiled=True, axis_index_groups=FAR)
    sums = jnp.sum(parts.reshape(QUADS, held, columns), axis=0)
    def step(total, moment, base):
        outer_grad = -total / lax.axis_size("rep")
        new_momentum = decay_rate * moment + outer_grad
        return new_momentum, base - outer_rate * (outer_grad + decay_rate * new_momentum)

    moment, base = moment.reshape(held, columns), base.reshape(held, columns)
    copies = lambda array: jnp.broadcast_to(array[None], (4 * LANES, held, columns))
    spread = step(copies(sums), copies(moment), copies(base))[1] * copies(scales)
    spread = spread.astype(jnp.bfloat16).reshape(rows, columns)
    encoded = lax.all_to_all(spread, "rep", 0, 0, tiled=True, axis_index_groups=BACK)
    encoded = encoded.reshape(LANES, 2, 2, QUADS, sub, columns).transpose(1, 3, 0, 2, 4, 5)
    encoded = jnp.concatenate([encoded[:, :, MIDDLE:], encoded[:, :, :MIDDLE]], axis=2).reshape(rows, columns)

    new_momentum, new_global = step(*[lax.dynamic_slice_in_dim(a, quad * sub, sub, 0) for a in (sums, moment, base)])
    key_grad = lax.dot_general(
        activations, key_cotangent, (((0,), (0,)), ((), ())), preferred_element_type=jnp.float32
    )
    key_grad = key_grad.astype(jnp.bfloat16)[None]
    return (key_grad, new_momentum, new_global, encoded)


def solution(mesh):
    in_specs = (
        P("rep", None),
        P("rep", "fsdp"),
        P("rep", None, "fsdp"),
        P("rep", None, "fsdp"),
        P(None, "fsdp"),
        P(None, "fsdp"),
        P(None, "fsdp"),
    )
    out_specs = (P("rep", None, "fsdp"), P("rep", "fsdp"), P("rep", "fsdp"), P(None, "fsdp"))
    return jax.shard_map(shards, mesh=mesh, in_specs=in_specs, out_specs=out_specs, check_vma=False)
```
